32 devices in a mesh: row: 8 (over z, core), col: 4 (over y, x).
Axes of the slice: x: 2, y: 2, z: 4, core: 2. Of those that a mesh axis runs over, the one named last changes fastest.
Arguments:
- gram: float32 [9, 512, 8, 2048], P(None, 'row', None, 'col'), may hold values from 0 to 4, as said below
Outputs:
- trailing: float32 [9, 512, 8, 2048], P(None, 'row', None, 'col')
- factor: float32 [8, 4, 512, 512], P(None, 'col', 'row')
The draws below stay inside these ranges and needn't reach their ends.
Inputs may be any that keep to these rules, and one draw needn't show every extreme that they name: gram holds the first 4608 rows of a symmetric positive definite 16384 x 16384 matrix whose smallest eigenvalue is at least 0.5.
All inputs are finite; a program needn't handle non-finite values.
Results may differ from the reference program's by a relative error of at most 0.0003.
Values sent between devices are 32-bit elements; how exact they have to be, the bound alone decides.
No kernel may reach another device: no remote copies, remote signals or barrier semaphores. Data moves between devices by JAX's collectives and lax.ppermute only.
A program may use at most 64 MiB of HBM per device.

```python
import jax
import jax.numpy as jnp
from jax import lax

B = 512
SLAB = 9
TC = 8
ORDER = 16384
N_COL = 4


def draw_gram(key, part):
    key_points, key_jitter = jax.random.split(key)
    point_dims = 16
    points = jax.random.normal(key_points, (ORDER, point_dims), jnp.float32)
    jitter = jax.random.uniform(key_jitter, (SLAB * B,), jnp.float32, 1.0, 2.0)
    distance = jnp.zeros((SLAB * B, ORDER), jnp.float32)
    for feature in range(point_dims):
        offset = points[:SLAB * B, None, feature] - points[None, :, feature]
        distance = distance + offset * offset
    kernel = jnp.exp(-distance / (2.0 * point_dims))
    row_index = jnp.arange(SLAB * B)
    col_index = jnp.arange(ORDER)
    kernel = jnp.where(row_index[:, None] == col_index[None, :], kernel + jitter[:, None], kernel)
    return kernel.reshape(SLAB, B, TC, ORDER // TC)


def setup_inputs(seed: int = 0) -> dict:
    arg_keys = jax.random.split(jax.random.key(seed), 2)
    gram = draw_gram(jax.random.fold_in(arg_keys[1], 71), 0)
    return {"gram": gram}


def reference(gram):
    matrix = gram.reshape(SLAB * B, ORDER)
    diagonal = matrix[:B, :B]
    factor_tile = jnp.linalg.cholesky(diagonal)
    inverse = jax.scipy.linalg.solve_triangular(factor_tile, jnp.eye(B, dtype=jnp.float32), lower=True)
    across = jnp.dot(matrix[:B, :].T, inverse.T, precision=lax.Precision.HIGHEST)
    across = across.at[:B].set(factor_tile)
    solved = jnp.dot(matrix[:, :B], inverse.T, precision=lax.Precision.HIGHEST)
    solved = solved.at[:B].set(factor_tile)
    product = jnp.dot(solved[B:], across[B:].T, precision=lax.Precision.HIGHEST)
    lower_part = matrix[B:, B:] - product
    trailing = jnp.pad(lower_part, ((B, 0), (B, 0)))
    return (trailing.reshape(SLAB, B, TC, ORDER // TC), across.reshape(TC, N_COL, B, B))
```

```python
import functools

import jax
import jax.numpy as jnp
from jax import lax
from jax.experimental import pallas as pl
from jax.experimental.pallas import tpu as pltpu
from jax.sharding import PartitionSpec as P

HIGHEST = lax.Precision.HIGHEST
SUBLANES = 8
LANES = 128
VMEM = pl.BlockSpec(memory_space=pltpu.VMEM)
ANY = pl.BlockSpec(memory_space=pl.ANY)
HBM = pl.BlockSpec(memory_space=pltpu.HBM)
SMEM = pl.BlockSpec(memory_space=pltpu.SMEM)


def f32(*shape):
    return jax.ShapeDtypeStruct(shape, jnp.float32)


def bf16(*shape):
    return jax.ShapeDtypeStruct(shape, jnp.bfloat16)


def call(kernel, out_shape, in_specs, out_specs, scratch=(), limit=16 << 20, aliases=None, micros=1):
    n_in, n_out = len(in_specs), len(out_specs)

    def with_token(_, *refs):
        refs[n_in + n_out][...] = jnp.zeros((SUBLANES, LANES), jnp.float32)
        kernel(*refs[: n_in + n_out], *refs[n_in + n_out + 1 :])

    return pl.pallas_call(
        with_token,
        out_shape=[*out_shape, f32(SUBLANES, LANES)],
        in_specs=[ANY, *in_specs],
        out_specs=[*out_specs, VMEM],
        scratch_shapes=list(scratch),
        input_output_aliases={i + 1: o for i, o in (aliases or {}).items()},
        cost_estimate=pl.CostEstimate(flops=int(micros * 5 * 10**7), bytes_accessed=0, transcendentals=0),
        compiler_params=pltpu.CompilerParams(vmem_limit_bytes=limit),
    )


def split(value):
    high = value.astype(jnp.bfloat16)
    return high, (value - high.astype(jnp.float32)).astype(jnp.bfloat16)


def dot3(a, b, dims=(((1,), (0,)), ((), ()))):
    dot = lambda x, y: lax.dot_general(x, y, dims, preferred_element_type=jnp.float32)
    return dot(a[0], b[0]) + (dot(a[0], b[1]) + dot(a[1], b[0]))


def prepare_kernel(order, held, chunks, diagonal):
    diagonal[...] = held[:, 0, :]
    for i, q in enumerate(order):
        for c in range(held.shape[1]):
            chunks[i, c] = held[:, c, q * LANES : (q + 1) * LANES]


def prepare(token, tile_row, order):
    part_rows, col_tiles, tile = tile_row.shape
    return call(
        functools.partial(prepare_kernel, order),
        [f32(len(order), col_tiles, part_rows, LANES), f32(part_rows, tile)],
        [VMEM],
        [VMEM] * 2,
        limit=8 << 20,
    )(token, tile_row)


def panel_kernel(place, gram, panel, held, sems):
    count = panel.shape[0]
    keep = place[2] == 0
    copies = [pltpu.make_async_copy(gram.at[a + 1], held.at[a % 4], sems.at[a % 4]) for a in range(count)]
    for a in range(min(4, count)):
        copies[a].start()
    for a in range(count):
        copies[a].wait()
        panel[a] = jnp.where(keep, held[a % 4, :, 0, :], 0.0)
        if a + 4 < count:
            copies[a + 4].start()


def take_panel(token, place, gram):
    slab, part_rows, col_tiles, tile = gram.shape
    return call(
        panel_kernel,
        [f32(slab - 1, part_rows, tile)],
        [SMEM, HBM],
        [VMEM],
        [pltpu.VMEM((4, part_rows, col_tiles, tile), jnp.float32), pltpu.SemaphoreType.DMA((4,))],
        limit=52 << 20,
        micros=4,
    )(token, place, gram)


def factor_block(groups):
    shape = (SUBLANES, LANES)
    sub = lax.broadcasted_iota(jnp.int32, shape, 0)
    lane = lax.broadcasted_iota(jnp.int32, shape, 1)
    row = lambda v, j: jnp.broadcast_to(v[j : j + 1, :], shape)
    col = lambda v, l: jnp.broadcast_to(v[:, l : l + 1], shape)
    groups = list(groups)
    upper, inverse = [], []
    for b in range(len(groups)):
        lo = SUBLANES * b
        panel = (lane >= lo) & (lane < lo + SUBLANES)
        rows_u = groups[b]
        rows_z = jnp.where(panel, jnp.where(lane == sub + lo, 1.0, 0.0), rows_u)
        columns = [col(rows_u, lo + j) for j in range(SUBLANES)]
        u_out, w_out, pivots = rows_u, rows_z, jnp.ones(shape, jnp.float32)
        for j in range(SUBLANES):
            pivot = row(columns[j], j)
            recip = 1.0 / pivot
            here = sub == j
            mult = jnp.where(here, 1.0 - recip, columns[j] * recip)
            z_row, u_row = row(rows_z, j), row(rows_u, j)
            u_out = jnp.where(here, u_row, u_out)
            w_out = jnp.where(here, z_row, w_out)
            pivots = jnp.where(here, pivot, pivots)
            for m in range(j + 1, SUBLANES):
                columns[m] = columns[m] - mult * row(columns[m], j)
            rows_z = rows_z - mult * z_row
            rows_u = rows_u - mult * u_row
        scale = lax.rsqrt(pivots)
        upper.append(jnp.where(lane >= lo + sub, u_out * scale, 0.0))
        inverse.append(jnp.where(lane <= lo + sub, w_out * scale, 0.0))
        z_rows = [row(rows_z, j) for j in range(SUBLANES)]
        for i in range(b + 1, len(groups)):
            g = groups[i]
            even = col(g, lo) * z_rows[0]
            odd = col(g, lo + 1) * z_rows[1]
            for j in range(2, SUBLANES, 2):
                even = even + col(g, lo + j) * z_rows[j]
                odd = odd + col(g, lo + j + 1) * z_rows[j + 1]
            groups[i] = jnp.where(panel, 0.0, g) - (even + odd)
    return upper, inverse


def block_step(p, n_blocks, state, u_ref):
    offset = pl.multiple_of(p * LANES, LANES)
    block = pl.ds(offset, LANES)
    groups = LANES // SUBLANES
    rows8 = [pl.ds(pl.multiple_of(offset + SUBLANES * i, SUBLANES), SUBLANES) for i in range(groups)]
    upper, inverse = factor_block([state[r, block] for r in rows8])
    for i in range(groups):
        u_ref[rows8[i], block] = upper[i]
        state[rows8[i], block] = inverse[i]
    own_inverse = state[block, block]

    def row_panel(i, _):
        at = pl.ds(pl.multiple_of(i * LANES, LANES), LANES)
        old = jnp.where(i == p, jnp.eye(LANES, dtype=jnp.float32), state[block, at])
        state[block, at] = jnp.dot(own_inverse, old, precision=HIGHEST, preferred_element_type=jnp.float32)
        return 0

    lax.fori_loop(0, n_blocks, row_panel, 0)

    def below(i, _):
        at = pl.ds(pl.multiple_of(i * LANES, LANES), LANES)
        coupling = state[block, at]
        u_ref[block, at] = coupling
        state[at, block] = jnp.zeros((LANES, LANES), jnp.float32)
        change = lax.dot_general(
            coupling, state[block, :], (((0,), (0,)), ((), ())), precision=HIGHEST, preferred_element_type=jnp.float32
        )
        state[at, :] = state[at, :] - change
        return 0

    lax.fori_loop(p + 1, n_blocks, below, 0)


def cholesky_kernel(first, last, n_own, n_z, place, *refs):
    if first == 0:
        own, other = refs[:n_own], refs[n_own : 2 * n_own]
        state, u_ref, sems = refs[2 * n_own :]
        z, core, c = place[0], place[1], place[2]
        rows = own[0].shape[0] // n_z
        copies = []
        for k, half in ((core, own), (1 - core, other)):
            for m, part in enumerate(half):
                for s in range(n_z):
                    zz = lax.rem(z - s + n_z, n_z)
                    at = ((zz * 2 + k) * n_own + lax.bitwise_xor(c, m)) * rows
                    copies.append(
                        pltpu.make_async_copy(
                            part.at[pl.ds(s * rows, rows), :],
                            state.at[pl.ds(pl.multiple_of(at, rows), rows), :],
                            sems.at[len(copies)],
                        )
                    )
        for copy in copies:
            copy.start()
        for copy in copies:
            copy.wait()
        u_ref[...] = jnp.zeros_like(u_ref)
    else:
        state_in, u_in, state, u_ref = refs
        state[...] = state_in[...]
        u_ref[...] = u_in[...]
    n_blocks = state.shape[0] // LANES

    def step(p, _):
        block_step(p, n_blocks, state, u_ref)
        return 0

    lax.fori_loop(first, last, step, 0)


def cholesky_start(token, place, own, other, tile, last, n_z):
    return call(
        functools.partial(cholesky_kernel, 0, last, len(own), n_z),
        [f32(tile, tile)] * 2,
        [SMEM] + [ANY] * (2 * len(own)),
        [VMEM] * 2,
        [pltpu.SemaphoreType.DMA((2 * len(own) * n_z,))],
        limit=8 << 20,
        micros=20,
    )(token, place, *own, *other)


def cholesky_next(token, place, state, first, last):
    return call(
        functools.partial(cholesky_kernel, first, last, 0, 0),
        [f32(*state[0].shape)] * 2,
        [SMEM, VMEM, VMEM],
        [VMEM] * 2,
        limit=8 << 20,
        micros=20 if last * LANES == state[0].shape[0] else 3,
    )(token, place, *state)


def weights_kernel(place, state, u_ref, *refs):
    n_parts = len(refs) - 6
    parts = refs[:n_parts]
    x_high, x_low, w_high, w_low, own_l, lower = refs[n_parts:]
    tile = state.shape[0]
    z, core, c = place[0], place[1], place[2]
    r = lax.broadcasted_iota(jnp.int32, (tile, tile), 0)
    s = lax.broadcasted_iota(jnp.int32, (tile, tile), 1)
    w = jnp.where(s <= r, state[...], 0.0)
    w_parts = split(w)
    w_high[...], w_low[...] = split(w.T)
    panel = jnp.concatenate([parts[i][...] + parts[i + 1][...] for i in range(0, n_parts, 2)], 0)
    g = dot3(split(panel), w_parts, (((1,), (1,)), ((), ())))
    x_high[...], x_low[...] = split(dot3(split(g), w_parts))
    part_rows = own_l.shape[0]
    lower[...] = u_ref[...].T
    own_l[...] = lower[pl.ds(pl.multiple_of((z * 2 + core) * part_rows, part_rows), part_rows), :]


def weights(token, place, state, upper, parts, part_rows):
    tile = state.shape[0]
    total = sum(part.shape[0] for part in parts) // 2
    return call(
        weights_kernel,
        [bf16(total, tile)] * 2 + [bf16(tile, tile)] * 2 + [f32(part_rows, tile)],
        [SMEM] + [VMEM] * (2 + len(parts)),
        [VMEM] * 5,
        [pltpu.VMEM((tile, tile), jnp.float32)],
    )(token, place, state, upper, *parts)


def update_kernel(q, slots_of, n_hops, place, gram, x_high, x_low, w_high, w_low, own_l, *refs):
    parts = [ref.at[i] for ref, i in zip(refs, slots_of)]
    own = parts[0]
    received = parts[1 : 1 + n_hops]
    swapped = parts[1 + n_hops : 1 + 2 * n_hops]
    rest = refs[1 + 2 * n_hops :]
    if q > 0:
        rest = rest[2:]
    trailing, factor, row0, old, new, fac, block_sems, old_sem, new_sems, fac_sem = rest
    z, core, c = place[0], place[1], place[2]
    n_z = n_hops + 1
    cores, col_tiles, part_rows, lanes = own.shape
    count = gram.shape[0] - 1
    tile = row0.shape[1]
    here = pl.ds(q * lanes, lanes)
    fetch = pltpu.make_async_copy(gram.at[pl.ds(1, count), :, :, here], old, old_sem)
    fetch.start()
    jobs = [(None, own, z)]
    for s in range(1, n_hops + 1):
        for below in (0, 1):
            zz = z - s if below == 0 else z + s
            inside = z >= s if below == 0 else z + s < n_z
            jobs.append((inside & (core == below), received[s - 1], zz))
            jobs.append((inside & (core != below), swapped[s - 1], zz))
    slots = 0
    actions = []
    for condition, source, zz in jobs:
        for k in range(cores):
            at = pl.multiple_of((zz * cores + k) * part_rows, part_rows)
            copy = pltpu.make_async_copy(source.at[k], row0.at[:, pl.ds(at, part_rows), :], block_sems.at[slots])
            slots += 1
            actions.append((condition, copy))
    for condition, copy in actions:
        if condition is None:
            copy.start()
        else:
            pl.when(condition)(copy.start)
    for condition, copy in actions:
        if condition is None:
            copy.wait()
        else:
            pl.when(condition)(copy.wait)

    first_col = c == 0
    columns = [split(jnp.concatenate([row0[t], row0[t + 1]], axis=1)) for t in range(0, col_tiles, 2)]
    old_zero = old.at[0]
    fetch.wait()
    out = []
    for half in range(2):
        first, last = count * half // 2, count * (half + 1) // 2
        rows = slice(first * part_rows, last * part_rows)
        x = (x_high[rows, :], x_low[rows, :])
        for i, column in enumerate(columns):
            product = dot3(x, column)
            for k in range(2):
                part = product[:, k * lanes : (k + 1) * lanes]
                new[first:last, :, 2 * i + k, :] = part.reshape(last - first, part_rows, lanes)
        for a in range(first, last):
            value = old[a] - new[a]
            sub = lax.broadcasted_iota(jnp.int32, value.shape, 1)
            new[a] = jnp.where(first_col & (sub == 0), 0.0, value)
        source, target = new.at[pl.ds(first, last - first)], trailing.at[pl.ds(1 + first, last - first), :, :, here]
        out.append(pltpu.make_async_copy(source, target, new_sems.at[half]))
        out[-1].start()
    old[0] = jnp.zeros(old.shape[1:], jnp.float32)
    out.append(pltpu.make_async_copy(old_zero, trailing.at[0, :, :, here], new_sems.at[2]))
    out[-1].start()

    mine = (z * cores + core) * part_rows

    @pl.when(mine // lanes == q)
    def _():
        at = pl.multiple_of(mine % lanes, part_rows)
        for t in range(col_tiles):
            fac[t] = row0[t].T
        across = fac[:, pl.ds(at, part_rows), :].reshape(col_tiles * part_rows, tile)
        value = dot3(split(across), (w_high[...], w_low[...])).reshape(col_tiles, part_rows, tile)
        fac[:, 0:part_rows, :] = value
        fac[0, 0:part_rows, :] = jnp.where(first_col, own_l[...], value[0])
        copy = pltpu.make_async_copy(fac.at[:, pl.ds(0, part_rows), :], factor.at[:, 0], fac_sem)
        copy.start()
        copy.wait()

    for copy in out:
        copy.wait()


def update(token, q, place, gram, weight, own, received, swapped, previous):
    slab, part_rows, col_tiles, tile = gram.shape
    n_hops = len(received)
    count = slab - 1
    parts = [own, *received, *swapped]
    slots_of = [i for _, i in parts]
    operands = [place, gram, *weight, *(array for array, _ in parts)]
    specs = [SMEM, HBM] + [VMEM] * 5 + [ANY] * (1 + 2 * n_hops)
    aliases = {}
    if previous is not None:
        aliases = {len(operands): 0, len(operands) + 1: 1}
        operands += list(previous)
        specs += [HBM] * 2
    scratch = [
        pltpu.VMEM((col_tiles, tile, LANES), jnp.float32),
        pltpu.VMEM((count, part_rows, col_tiles, LANES), jnp.float32),
        pltpu.VMEM((count, part_rows, col_tiles, LANES), jnp.float32),
        pltpu.VMEM((col_tiles, LANES, tile), jnp.float32),
        pltpu.SemaphoreType.DMA((2 * (1 + 4 * n_hops),)),
        pltpu.SemaphoreType.DMA,
        pltpu.SemaphoreType.DMA((3,)),
        pltpu.SemaphoreType.DMA,
    ]
    return call(
        functools.partial(update_kernel, q, slots_of, n_hops),
        [f32(*gram.shape), f32(col_tiles, 1, part_rows, tile)],
        specs,
        [HBM, HBM],
        scratch,
        limit=30 << 20,
        micros=2,
        aliases=aliases,
    )(token, *operands)


def scatter(parts, root, axis):
    here = lax.axis_index(axis) == root
    mine = jnp.where(here, parts[0], 0.0)
    sent = [lax.ppermute(part, axis, [(root, i)]) for i, part in enumerate(parts) if i != root]
    return functools.reduce(jnp.add, sent, mine)


def exchange(part, axis, size):
    return [part] + [lax.ppermute(part, axis, [(i, i ^ m) for i in range(size)]) for m in range(1, size)]


def together(*values):
    return lax.optimization_barrier(values)


def body(gram, rows, cols):
    slab, part_rows, col_tiles, tile = gram.shape
    n_z = rows // 2
    n_chunks = tile // LANES
    n_blocks = tile // LANES
    core = lax.axis_index("row") % 2
    place = jnp.stack([lax.axis_index("row") // 2, core, lax.axis_index("col")]).astype(jnp.int32)
    other_core = [(i, i ^ 1) for i in range(rows)]
    swap = lambda value: lax.ppermute(value, "row", other_core)
    spread = lambda value, level: lax.ppermute(value, "col", [(i, i + level) for i in range(level)])

    def hop(value, s):
        pairs = [(2 * z, 2 * z + 2) for z in range(s - 1, n_z - 1)]
        pairs += [(2 * z + 1, 2 * z - 1) for z in range(1, n_z - s + 1)]
        return lax.ppermute(value, "row", pairs)

    order = sorted(range(n_chunks), key=lambda q: -abs(2 * q - n_chunks + 1))
    token = jnp.zeros((SUBLANES, LANES), jnp.float32)
    chunks, diagonal, token = prepare(token, gram[0], order)
    share = part_rows // cols
    piece = scatter([diagonal[i * share : (i + 1) * share] for i in range(cols)], 0, "col")
    partner = swap(chunks)
    blocks = jnp.stack([jnp.where(core == 0, chunks, partner), jnp.where(core == 0, partner, chunks)], 1)

    piece, blocks = together(piece, blocks)
    ring = [piece]
    for s in range(1, n_z):
        ring.append(lax.ppermute(piece, "row", [(i, (i + 2 * s) % rows) for i in range(rows)]))
    piece = jnp.concatenate(ring, 0)
    piece, blocks, token = together(piece, blocks, token)
    hops = [hop(blocks, 1)]
    halves = exchange(piece, "col", cols)
    panel, token = take_panel(token, place, gram)
    token, panel, *halves = together(token, panel, *halves)
    others = [swap(half) for half in halves]

    panel = panel.reshape((slab - 1) * part_rows, tile)
    half = panel.shape[0] // 2
    parts = [[panel[i * half : (i + 1) * half]] for i in range(2)]
    parts[0].append(spread(parts[0][0], 1))
    *state, token = cholesky_start(token, place, halves, others, tile, 1, n_z)
    token, parts[0][1], parts[1][0], hops[0] = together(token, parts[0][1], parts[1][0], hops[0])
    for s in range(2, n_z - 1):
        hops.append(hop(hops[-1], s))
    parts[1].append(spread(parts[1][0], 1))
    levels = cols.bit_length() - 1
    for level in range(1, levels):
        total = parts[0][0] + parts[0][1]
        parts[0] = [total, spread(total, 1 << level)]
    for p in range(1, n_blocks):
        if p == n_blocks - 1:
            token, parts[0][1], parts[1][1] = together(token, parts[0][1], parts[1][1])
            for level in range(1, levels):
                total = parts[1][0] + parts[1][1]
                parts[1] = [total, spread(total, 1 << level)]
        *state, token = cholesky_next(token, place, state, p, p + 1)
    parts = [value for pair in parts for value in pair]
    token, parts[-1], *hops = together(token, parts[-1], *hops)
    *weight, token = weights(token, place, *state, parts, part_rows)

    swapped = [swap(value) for value in hops]
    finals = [hop(hops[-1][i : i + 1], n_z - 1) for i in range(n_chunks)]
    outs = None
    for i, q in enumerate(order):
        if 0 < i < n_chunks - 1:
            token, finals[i + 1] = together(token, finals[i + 1])
        received = [(value, i) for value in hops] + [(finals[i], 0)]
        others = [(value, i) for value in swapped] + [(swap(finals[i]), 0)]
        *outs, token = update(token, q, place, gram, weight, (blocks, i), received, others, outs)
    return tuple(outs)


def solution(mesh):
    rows, cols = mesh.shape["row"], mesh.shape["col"]
    return jax.shard_map(
        functools.partial(body, rows=rows, cols=cols),
        mesh=mesh,
        in_specs=(P(None, "row", None, "col"),),
        out_specs=(P(None, "row", None, "col"), P(None, "col", "row", None)),
        check_vma=False,
    )
```

```python
import functools

import jax
import jax.numpy as jnp
from jax import lax
from jax.experimental import pallas as pl
from jax.experimental.pallas import tpu as pltpu
from jax.sharding import PartitionSpec as P

HIGHEST = lax.Precision.HIGHEST
SUBLANES = 8
LANES = 128
VMEM = pl.BlockSpec(memory_space=pltpu.VMEM)
ANY = pl.BlockSpec(memory_space=pl.ANY)
HBM = pl.BlockSpec(memory_space=pltpu.HBM)
SMEM = pl.BlockSpec(memory_space=pltpu.SMEM)


def f32(*shape):
    return jax.ShapeDtypeStruct(shape, jnp.float32)


def bf16(*shape):
    return jax.ShapeDtypeStruct(shape, jnp.bfloat16)


def call(kernel, out_shape, in_specs, out_specs, scratch=(), limit=16 << 20, aliases=None, micros=1):
    n_in, n_out = len(in_specs), len(out_specs)

    def with_token(_, *refs):
        refs[n_in + n_out][...] = jnp.zeros((SUBLANES, LANES), jnp.float32)
        kernel(*refs[: n_in + n_out], *refs[n_in + n_out + 1 :])

    return pl.pallas_call(
        with_token,
        out_shape=[*out_shape, f32(SUBLANES, LANES)],
        in_specs=[ANY, *in_specs],
        out_specs=[*out_specs, VMEM],
        scratch_shapes=list(scratch),
        input_output_aliases={i + 1: o for i, o in (aliases or {}).items()},
        cost_estimate=pl.CostEstimate(flops=int(micros * 5 * 10**7), bytes_accessed=0, transcendentals=0),
        compiler_params=pltpu.CompilerParams(vmem_limit_bytes=limit),
    )


def split(value):
    high = value.astype(jnp.bfloat16)
    return high, (value - high.astype(jnp.float32)).astype(jnp.bfloat16)


def dot3(a, b, dims=(((1,), (0,)), ((), ()))):
    dot = lambda x, y: lax.dot_general(x, y, dims, preferred_element_type=jnp.float32)
    return dot(a[0], b[0]) + (dot(a[0], b[1]) + dot(a[1], b[0]))


def prepare_kernel(order, held, chunks, diagonal):
    diagonal[...] = held[:, 0, :]
    for i, q in enumerate(order):
        for c in range(held.shape[1]):
            chunks[i, c] = held[:, c, q * LANES : (q + 1) * LANES]


def prepare(token, tile_row, order):
    part_rows, col_tiles, tile = tile_row.shape
    return call(
        functools.partial(prepare_kernel, order),
        [f32(len(order), col_tiles, part_rows, LANES), f32(part_rows, tile)],
        [VMEM],
        [VMEM] * 2,
        limit=8 << 20,
    )(token, tile_row)


def panel_kernel(place, gram, panel, held, sems):
    count = panel.shape[0]
    keep = place[2] == 0
    copies = [pltpu.make_async_copy(gram.at[a + 1], held.at[a % 4], sems.at[a % 4]) for a in range(count)]
    for a in range(min(4, count)):
        copies[a].start()
    for a in range(count):
        copies[a].wait()
        panel[a] = jnp.where(keep, held[a % 4, :, 0, :], 0.0)
        if a + 4 < count:
            copies[a + 4].start()


def take_panel(token, place, gram):
    slab, part_rows, col_tiles, tile = gram.shape
    return call(
        panel_kernel,
        [f32(slab - 1, part_rows, tile)],
        [SMEM, HBM],
        [VMEM],
        [pltpu.VMEM((4, part_rows, col_tiles, tile), jnp.float32), pltpu.SemaphoreType.DMA((4,))],
        limit=52 << 20,
        micros=4,
    )(token, place, gram)


def factor_block(groups):
    shape = (SUBLANES, LANES)
    sub = lax.broadcasted_iota(jnp.int32, shape, 0)
    lane = lax.broadcasted_iota(jnp.int32, shape, 1)
    row = lambda v, j: jnp.broadcast_to(v[j : j + 1, :], shape)
    col = lambda v, l: jnp.broadcast_to(v[:, l : l + 1], shape)
    groups = list(groups)
    upper, inverse = [], []
    for b in range(len(groups)):
        lo = SUBLANES * b
        panel = (lane >= lo) & (lane < lo + SUBLANES)
        rows_u = groups[b]
        rows_z = jnp.where(panel, jnp.where(lane == sub + lo, 1.0, 0.0), rows_u)
        columns = [col(rows_u, lo + j) for j in range(SUBLANES)]
        u_out, w_out, pivots = rows_u, rows_z, jnp.ones(shape, jnp.float32)
        for j in range(SUBLANES):
            pivot = row(columns[j], j)
            recip = 1.0 / pivot
            here = sub == j
            mult = jnp.where(here, 1.0 - recip, columns[j] * recip)
            z_row, u_row = row(rows_z, j), row(rows_u, j)
            u_out = jnp.where(here, u_row, u_out)
            w_out = jnp.where(here, z_row, w_out)
            pivots = jnp.where(here, pivot, pivots)
            for m in range(j + 1, SUBLANES):
                columns[m] = columns[m] - mult * row(columns[m], j)
            rows_z = rows_z - mult * z_row
            rows_u = rows_u - mult * u_row
        scale = lax.rsqrt(pivots)
        upper.append(jnp.where(lane >= lo + sub, u_out * scale, 0.0))
        inverse.append(jnp.where(lane <= lo + sub, w_out * scale, 0.0))
        z_rows = [row(rows_z, j) for j in range(SUBLANES)]
        for i in range(b + 1, len(groups)):
            g = groups[i]
            even = col(g, lo) * z_rows[0]
            odd = col(g, lo + 1) * z_rows[1]
            for j in range(2, SUBLANES, 2):
                even = even + col(g, lo + j) * z_rows[j]
                odd = odd + col(g, lo + j + 1) * z_rows[j + 1]
            groups[i] = jnp.where(panel, 0.0, g) - (even + odd)
    return upper, inverse


def block_step(p, n_blocks, state, u_ref):
    offset = pl.multiple_of(p * LANES, LANES)
    block = pl.ds(offset, LANES)
    groups = LANES // SUBLANES
    rows8 = [pl.ds(pl.multiple_of(offset + SUBLANES * i, SUBLANES), SUBLANES) for i in range(groups)]
    upper, inverse = factor_block([state[r, block] for r in rows8])
    for i in range(groups):
        u_ref[rows8[i], block] = upper[i]
        state[rows8[i], block] = inverse[i]
    own_inverse = state[block, block]

    def row_panel(i, _):
        at = pl.ds(pl.multiple_of(i * LANES, LANES), LANES)
        old = jnp.where(i == p, jnp.eye(LANES, dtype=jnp.float32), state[block, at])
        state[block, at] = jnp.dot(own_inverse, old, precision=HIGHEST, preferred_element_type=jnp.float32)
        return 0

    lax.fori_loop(0, n_blocks, row_panel, 0)

    def below(i, _):
        at = pl.ds(pl.multiple_of(i * LANES, LANES), LANES)
        coupling = state[block, at]
        u_ref[block, at] = coupling
        state[at, block] = jnp.zeros((LANES, LANES), jnp.float32)
        change = lax.dot_general(
            coupling, state[block, :], (((0,), (0,)), ((), ())), precision=HIGHEST, preferred_element_type=jnp.float32
        )
        state[at, :] = state[at, :] - change
        return 0

    lax.fori_loop(p + 1, n_blocks, below, 0)


def cholesky_kernel(first, last, n_own, n_z, place, *refs):
    if first == 0:
        own, other = refs[:n_own], refs[n_own : 2 * n_own]
        state, u_ref, sems = refs[2 * n_own :]
        z, core, c = place[0], place[1], place[2]
        rows = own[0].shape[0] // n_z
        copies = []
        for k, half in ((core, own), (1 - core, other)):
            for m, part in enumerate(half):
                for s in range(n_z):
                    zz = lax.rem(z - s + n_z, n_z)
                    at = ((zz * 2 + k) * n_own + lax.bitwise_xor(c, m)) * rows
                    copies.append(
                        pltpu.make_async_copy(
                            part.at[pl.ds(s * rows, rows), :],
                            state.at[pl.ds(pl.multiple_of(at, rows), rows), :],
                            sems.at[len(copies)],
                        )
                    )
        for copy in copies:
            copy.start()
        for copy in copies:
            copy.wait()
        u_ref[...] = jnp.zeros_like(u_ref)
    else:
        state_in, u_in, state, u_ref = refs
        state[...] = state_in[...]
        u_ref[...] = u_in[...]
    n_blocks = state.shape[0] // LANES

    def step(p, _):
        block_step(p, n_blocks, state, u_ref)
        return 0

    lax.fori_loop(first, last, step, 0)


def cholesky_start(token, place, own, other, tile, last, n_z):
    return call(
        functools.partial(cholesky_kernel, 0, last, len(own), n_z),
        [f32(tile, tile)] * 2,
        [SMEM] + [ANY] * (2 * len(own)),
        [VMEM] * 2,
        [pltpu.SemaphoreType.DMA((2 * len(own) * n_z,))],
        limit=8 << 20,
        micros=60,
    )(token, place, *own, *other)


def cholesky_next(token, place, state, first, last):
    return call(
        functools.partial(cholesky_kernel, first, last, 0, 0),
        [f32(*state[0].shape)] * 2,
        [SMEM, VMEM, VMEM],
        [VMEM] * 2,
        limit=8 << 20,
        micros=20,
    )(token, place, *state)


def weights_kernel(place, state, u_ref, *refs):
    n_parts = len(refs) - 6
    parts = refs[:n_parts]
    x_high, x_low, w_high, w_low, own_l, lower = refs[n_parts:]
    tile = state.shape[0]
    z, core, c = place[0], place[1], place[2]
    r = lax.broadcasted_iota(jnp.int32, (tile, tile), 0)
    s = lax.broadcasted_iota(jnp.int32, (tile, tile), 1)
    w = jnp.where(s <= r, state[...], 0.0)
    w_parts = split(w)
    w_high[...], w_low[...] = split(w.T)
    panel = jnp.concatenate([parts[i][...] + parts[i + 1][...] for i in range(0, n_parts, 2)], 0)
    g = dot3(split(panel), w_parts, (((1,), (1,)), ((), ())))
    x_high[...], x_low[...] = split(dot3(split(g), w_parts))
    part_rows = own_l.shape[0]
    lower[...] = u_ref[...].T
    own_l[...] = lower[pl.ds(pl.multiple_of((z * 2 + core) * part_rows, part_rows), part_rows), :]


def weights(token, place, state, upper, parts, part_rows):
    tile = state.shape[0]
    total = sum(part.shape[0] for part in parts) // 2
    return call(
        weights_kernel,
        [bf16(total, tile)] * 2 + [bf16(tile, tile)] * 2 + [f32(part_rows, tile)],
        [SMEM] + [VMEM] * (2 + len(parts)),
        [VMEM] * 5,
        [pltpu.VMEM((tile, tile), jnp.float32)],
    )(token, place, state, upper, *parts)


def own_columns(row0, fac, at, part_rows):
    col_tiles, depth = row0.shape[0], row0.shape[1]
    for t in range(col_tiles):
        fac[t, :, 0:depth] = row0[t].T
    return fac[:, pl.ds(at, part_rows), 0:depth].reshape(col_tiles * part_rows, depth)


def update_kernel(chunks, starts, n_hops, place, gram, x_high, x_low, w_high, w_low, own_l, *refs):
    sources, rest = refs[: 1 + 2 * n_hops], refs[1 + 2 * n_hops :]
    trailing, factor, row0, old, new, zero, fac, prod, block_sems, old_sems, new_sems, zero_sems, fac_sem = rest[-13:]
    z, core, c = place[0], place[1], place[2]
    n_z = n_hops + 1
    _, cores, col_tiles, part_rows, lanes = sources[0].shape
    count, tile = old.shape[1], row0.shape[2]
    first_col = c == 0
    x = (x_high[...], x_low[...])

    def transfers(i):
        position, q = chunks[i]
        slot, here = i % 2, pl.ds(q * lanes, lanes)
        jobs = [(None, 0, z)]
        for s in range(1, n_hops + 1):
            for below, zz, inside in ((0, z - s, z >= s), (1, z + s, z + s < n_z)):
                jobs.append((inside & (core == below), s, zz))
                jobs.append((inside & (core != below), n_hops + s, zz))
        found = [(None, pltpu.make_async_copy(gram.at[pl.ds(1, count), :, :, here], old.at[slot], old_sems.at[slot]))]
        for job, (condition, source, zz) in enumerate(jobs):
            for k in range(cores):
                at = pl.multiple_of((zz * cores + k) * part_rows, part_rows)
                origin = sources[source].at[position - starts[source], k]
                target = row0.at[slot, :, pl.ds(at, part_rows), :]
                found.append((condition, pltpu.make_async_copy(origin, target, block_sems.at[slot, job, k])))
        return found

    def each(i, action):
        for condition, copy in transfers(i):
            if condition is None:
                action(copy)
            else:
                pl.when(condition)(functools.partial(action, copy))

    each(0, lambda copy: copy.start())
    zero[...] = jnp.zeros(zero.shape, jnp.float32)
    zeros = [
        pltpu.make_async_copy(zero, trailing.at[0, :, :, pl.ds(q * lanes, lanes)], zero_sems.at[i])
        for i, (_, q) in enumerate(chunks)
    ]
    outs = []
    mine = (z * cores + core) * part_rows
    place_factor = pltpu.make_async_copy(fac.at[:, pl.ds(0, part_rows), :], factor.at[:, 0], fac_sem)
    owner = [mine // lanes == q for _, q in chunks]
    for i, (_, q) in enumerate(chunks):
        slot, here = i % 2, pl.ds(q * lanes, lanes)
        if i + 1 < len(chunks):
            each(i + 1, lambda copy: copy.start())
        each(i, lambda copy: copy.wait())
        if i == 0:
            for copy in zeros:
                copy.start()
        if i >= 2:
            outs[i - 2].wait()
        for t in range(0, col_tiles, 2):
            column = split(jnp.concatenate([row0[slot, t], row0[slot, t + 1]], axis=1))
            product = dot3(x, column)
            prod[t] = product[:, :LANES]
            prod[t + 1] = product[:, LANES:]
        sub = lax.broadcasted_iota(jnp.int32, (part_rows, col_tiles, LANES), 1)
        for a in range(count):
            part = jnp.swapaxes(prod[:, a * part_rows : (a + 1) * part_rows, :], 0, 1)
            new[slot, a] = jnp.where(first_col & (sub == 0), 0.0, old[slot, a] - part)
        outs.append(
            pltpu.make_async_copy(new.at[slot], trailing.at[pl.ds(1, count), :, :, here], new_sems.at[slot])
        )
        outs[i].start()

        @pl.when(owner[i])
        def _():
            at = pl.multiple_of(mine % lanes, part_rows)
            across = own_columns(row0.at[slot], fac, at, part_rows)
            value = dot3(split(across), (w_high[...], w_low[...])).reshape(col_tiles, part_rows, tile)
            fac[:, 0:part_rows, :] = value
            fac[0, 0:part_rows, :] = jnp.where(first_col, own_l[...], value[0])
            place_factor.start()

    for is_owner in owner:
        pl.when(is_owner)(place_factor.wait)
    for copy in outs[-2:] + zeros:
        copy.wait()


def update(token, chunks, place, gram, weight, sources, previous):
    slab, part_rows, col_tiles, tile = gram.shape
    n_hops = (len(sources) - 1) // 2
    count = slab - 1
    operands = [place, gram, *weight, *(array for array, _ in sources)]
    specs = [SMEM, HBM] + [VMEM] * 5 + [ANY] * len(sources)
    aliases = {}
    if previous is not None:
        aliases = {len(operands): 0, len(operands) + 1: 1}
        operands += list(previous)
        specs += [HBM] * 2
    slots = pltpu.VMEM((2, count, part_rows, col_tiles, LANES), jnp.float32)
    scratch = [
        pltpu.VMEM((2, col_tiles, tile, LANES), jnp.float32),
        slots,
        slots,
        pltpu.VMEM((part_rows, col_tiles, LANES), jnp.float32),
        pltpu.VMEM((col_tiles, LANES, tile), jnp.float32),
        pltpu.VMEM((col_tiles, count * part_rows, LANES), jnp.float32),
        pltpu.SemaphoreType.DMA((2, 1 + 4 * n_hops, 2)),
        pltpu.SemaphoreType.DMA((2,)),
        pltpu.SemaphoreType.DMA((2,)),
        pltpu.SemaphoreType.DMA((len(chunks),)),
        pltpu.SemaphoreType.DMA,
    ]
    return call(
        functools.partial(update_kernel, chunks, [start for _, start in sources], n_hops),
        [f32(*gram.shape), f32(col_tiles, 1, part_rows, tile)],
        specs,
        [HBM, HBM],
        scratch,
        limit=26 << 20,
        micros=0,
        aliases=aliases,
    )(token, *operands)


def scatter(parts, root, axis):
    here = lax.axis_index(axis) == root
    mine = jnp.where(here, parts[0], 0.0)
    sent = [lax.ppermute(part, axis, [(root, i)]) for i, part in enumerate(parts) if i != root]
    return functools.reduce(jnp.add, sent, mine)


def exchange(part, axis, size):
    return [part] + [lax.ppermute(part, axis, [(i, i ^ m) for i in range(size)]) for m in range(1, size)]


def together(*values):
    return lax.optimization_barrier(values)


def body(gram, rows, cols):
    slab, part_rows, col_tiles, tile = gram.shape
    n_z = rows // 2
    n_chunks = tile // LANES
    n_blocks = tile // LANES
    core = lax.axis_index("row") % 2
    place = jnp.stack([lax.axis_index("row") // 2, core, lax.axis_index("col")]).astype(jnp.int32)
    other_core = [(i, i ^ 1) for i in range(rows)]
    swap = lambda value: lax.ppermute(value, "row", other_core)
    spread = lambda value, level: lax.ppermute(value, "col", [(i, i + level) for i in range(level)])

    def hop(value, s):
        pairs = [(2 * z, 2 * z + 2) for z in range(s - 1, n_z - 1)]
        pairs += [(2 * z + 1, 2 * z - 1) for z in range(1, n_z - s + 1)]
        return lax.ppermute(value, "row", pairs)

    order = sorted(range(n_chunks), key=lambda q: -abs(2 * q - n_chunks + 1))
    token = jnp.zeros((SUBLANES, LANES), jnp.float32)
    chunks, diagonal, token = prepare(token, gram[0], order)
    share = part_rows // cols
    piece = scatter([diagonal[i * share : (i + 1) * share] for i in range(cols)], 0, "col")
    partner = swap(chunks)
    blocks = jnp.stack([jnp.where(core == 0, chunks, partner), jnp.where(core == 0, partner, chunks)], 1)

    piece, blocks, token = together(piece, blocks, token)
    ring = [piece]
    for s in range(1, n_z):
        ring.append(lax.ppermute(piece, "row", [(i, (i + 2 * s) % rows) for i in range(rows)]))
    piece = jnp.concatenate(ring, 0)
    panel, token = take_panel(token, place, gram)
    panel = panel.reshape((slab - 1) * part_rows, tile)
    levels = cols.bit_length() - 1
    piece, blocks, token = together(piece, blocks, token)
    hops = [hop(blocks, 1)]
    halves = exchange(piece, "col", cols)
    panel, *halves = together(panel, *halves)
    others = [swap(half) for half in halves]

    height = panel.shape[0]
    bounds = [0, height * 2 // 5 // SUBLANES * SUBLANES, height * 7 // 10 // SUBLANES * SUBLANES, height]
    held = [panel[first:last] for first, last in zip(bounds[:-1], bounds[1:])]
    sent = [None] * len(held)

    def launch(step):
        moving = [i for i in range(len(held)) if 0 <= step - i < levels]
        for i in moving:
            if step > i:
                held[i] = held[i] + sent[i]
            sent[i] = spread(held[i], 1 << (step - i))
        return moving

    for p in range(n_blocks):
        moving = launch(p)
        if p == 0:
            *state, token = cholesky_start(token, place, halves, others, tile, 1, n_z)
        else:
            if p == n_blocks - 1:
                token, *hops = together(token, *hops)
            *state, token = cholesky_next(token, place, state, p, p + 1)
        if p == 0:
            token, hops[0], sent[0] = together(token, hops[0], sent[0])
            for s in range(2, n_z - 1):
                hops.append(hop(hops[-1], s))
        else:
            token, *landed = together(token, *(sent[i] for i in moving))
            for i, value in zip(moving, landed):
                sent[i] = value
    for step in range(n_blocks, len(held) + levels - 1):
        launch(step)
    parts = [value for pair in zip(held, sent) for value in pair]
    swapped = [swap(value) for value in hops]

    pair = n_chunks // 2
    finals = [hop(hops[-1][i : i + pair], n_z - 1) for i in (0, pair)]
    *weight, token = weights(token, place, *state, parts, part_rows)
    outs = None
    for final, first in zip(finals, (0, pair)):
        token, final = together(token, final)
        sources = [(value, 0) for value in (blocks, *hops)] + [(final, first)]
        sources += [(value, 0) for value in swapped] + [(swap(final), first)]
        positions = [(i, order[i]) for i in range(first, first + pair)]
        *outs, token = update(token, positions, place, gram, weight, sources, outs)
    return tuple(outs)


def solution(mesh):
    rows, cols = mesh.shape["row"], mesh.shape["col"]
    return jax.shard_map(
        functools.partial(body, rows=rows, cols=cols),
        mesh=mesh,
        in_specs=(P(None, "row", None, "col"),),
        out_specs=(P(None, "row", None, "col"), P(None, "col", "row", None)),
        check_vma=False,
    )
```

```python
import functools

import jax
import jax.numpy as jnp
from jax import lax
from jax.experimental import pallas as pl
from jax.experimental.pallas import tpu as pltpu
from jax.sharding import PartitionSpec as P

HIGHEST = lax.Precision.HIGHEST
SUBLANES = 8
LANES = 128
VMEM = pl.BlockSpec(memory_space=pltpu.VMEM)
ANY = pl.BlockSpec(memory_space=pl.ANY)
HBM = pl.BlockSpec(memory_space=pltpu.HBM)
SMEM = pl.BlockSpec(memory_space=pltpu.SMEM)


def f32(*shape):
    return jax.ShapeDtypeStruct(shape, jnp.float32)


def bf16(*shape):
    return jax.ShapeDtypeStruct(shape, jnp.bfloat16)


def call(kernel, out_shape, in_specs, out_specs, scratch=(), limit=16 << 20, aliases=None, micros=1):
    n_in, n_out = len(in_specs), len(out_specs)

    def with_token(_, *refs):
        refs[n_in + n_out][...] = jnp.zeros((SUBLANES, LANES), jnp.float32)
        kernel(*refs[: n_in + n_out], *refs[n_in + n_out + 1 :])

    return pl.pallas_call(
        with_token,
        out_shape=[*out_shape, f32(SUBLANES, LANES)],
        in_specs=[ANY, *in_specs],
        out_specs=[*out_specs, VMEM],
        scratch_shapes=list(scratch),
        input_output_aliases={i + 1: o for i, o in (aliases or {}).items()},
        cost_estimate=pl.CostEstimate(flops=int(micros * 5 * 10**7), bytes_accessed=0, transcendentals=0),
        compiler_params=pltpu.CompilerParams(vmem_limit_bytes=limit),
    )


def split(value):
    high = value.astype(jnp.bfloat16)
    return high, (value - high.astype(jnp.float32)).astype(jnp.bfloat16)


def dot3(a, b, dims=(((1,), (0,)), ((), ()))):
    dot = lambda x, y: lax.dot_general(x, y, dims, preferred_element_type=jnp.float32)
    return dot(a[0], b[0]) + (dot(a[0], b[1]) + dot(a[1], b[0]))


def prepare_kernel(order, held, chunks, diagonal):
    diagonal[...] = held[:, 0, :]
    for i, q in enumerate(order):
        for c in range(held.shape[1]):
            chunks[i, c] = held[:, c, q * LANES : (q + 1) * LANES]


def prepare(token, tile_row, order):
    part_rows, col_tiles, tile = tile_row.shape
    return call(
        functools.partial(prepare_kernel, order),
        [f32(len(order), col_tiles, part_rows, LANES), f32(part_rows, tile)],
        [VMEM],
        [VMEM] * 2,
        limit=8 << 20,
    )(token, tile_row)


def panel_kernel(place, gram, panel, held, sems):
    count = panel.shape[0]
    keep = place[2] == 0
    copies = [pltpu.make_async_copy(gram.at[a + 1], held.at[a % 4], sems.at[a % 4]) for a in range(count)]
    for a in range(min(4, count)):
        copies[a].start()
    for a in range(count):
        copies[a].wait()
        panel[a] = jnp.where(keep, held[a % 4, :, 0, :], 0.0)
        if a + 4 < count:
            copies[a + 4].start()


def take_panel(token, place, gram):
    slab, part_rows, col_tiles, tile = gram.shape
    return call(
        panel_kernel,
        [f32(slab - 1, part_rows, tile)],
        [SMEM, HBM],
        [VMEM],
        [pltpu.VMEM((4, part_rows, col_tiles, tile), jnp.float32), pltpu.SemaphoreType.DMA((4,))],
        limit=52 << 20,
        micros=4,
    )(token, place, gram)


def factor_block(groups):
    shape = (SUBLANES, LANES)
    sub = lax.broadcasted_iota(jnp.int32, shape, 0)
    lane = lax.broadcasted_iota(jnp.int32, shape, 1)
    row = lambda v, j: jnp.broadcast_to(v[j : j + 1, :], shape)
    col = lambda v, l: jnp.broadcast_to(v[:, l : l + 1], shape)
    groups = list(groups)
    upper, inverse = [], []
    for b in range(len(groups)):
        lo = SUBLANES * b
        panel = (lane >= lo) & (lane < lo + SUBLANES)
        rows_u = groups[b]
        rows_z = jnp.where(panel, jnp.where(lane == sub + lo, 1.0, 0.0), rows_u)
        columns = [col(rows_u, lo + j) for j in range(SUBLANES)]
        u_out, w_out, pivots = rows_u, rows_z, jnp.ones(shape, jnp.float32)
        for j in range(SUBLANES):
            pivot = row(columns[j], j)
            recip = 1.0 / pivot
            here = sub == j
            mult = jnp.where(here, 1.0 - recip, columns[j] * recip)
            z_row, u_row = row(rows_z, j), row(rows_u, j)
            u_out = jnp.where(here, u_row, u_out)
            w_out = jnp.where(here, z_row, w_out)
            pivots = jnp.where(here, pivot, pivots)
            for m in range(j + 1, SUBLANES):
                columns[m] = columns[m] - mult * row(columns[m], j)
            rows_z = rows_z - mult * z_row
            rows_u = rows_u - mult * u_row
        scale = lax.rsqrt(pivots)
        upper.append(jnp.where(lane >= lo + sub, u_out * scale, 0.0))
        inverse.append(jnp.where(lane <= lo + sub, w_out * scale, 0.0))
        z_rows = [row(rows_z, j) for j in range(SUBLANES)]
        for i in range(b + 1, len(groups)):
            g = groups[i]
            even = col(g, lo) * z_rows[0]
            odd = col(g, lo + 1) * z_rows[1]
            for j in range(2, SUBLANES, 2):
                even = even + col(g, lo + j) * z_rows[j]
                odd = odd + col(g, lo + j + 1) * z_rows[j + 1]
            groups[i] = jnp.where(panel, 0.0, g) - (even + odd)
    return upper, inverse


def block_step(p, n_blocks, state, u_ref):
    offset = pl.multiple_of(p * LANES, LANES)
    block = pl.ds(offset, LANES)
    groups = LANES // SUBLANES
    rows8 = [pl.ds(pl.multiple_of(offset + SUBLANES * i, SUBLANES), SUBLANES) for i in range(groups)]
    upper, inverse = factor_block([state[r, block] for r in rows8])
    for i in range(groups):
        u_ref[rows8[i], block] = upper[i]
        state[rows8[i], block] = inverse[i]
    own_inverse = state[block, block]

    def row_panel(i, _):
        at = pl.ds(pl.multiple_of(i * LANES, LANES), LANES)
        old = jnp.where(i == p, jnp.eye(LANES, dtype=jnp.float32), state[block, at])
        state[block, at] = jnp.dot(own_inverse, old, precision=HIGHEST, preferred_element_type=jnp.float32)
        return 0

    lax.fori_loop(0, n_blocks, row_panel, 0)

    def below(i, _):
        at = pl.ds(pl.multiple_of(i * LANES, LANES), LANES)
        coupling = state[block, at]
        u_ref[block, at] = coupling
        state[at, block] = jnp.zeros((LANES, LANES), jnp.float32)
        change = lax.dot_general(
            coupling, state[block, :], (((0,), (0,)), ((), ())), precision=HIGHEST, preferred_element_type=jnp.float32
        )
        state[at, :] = state[at, :] - change
        return 0

    lax.fori_loop(p + 1, n_blocks, below, 0)


def cholesky_kernel(first, last, n_own, n_z, place, *refs):
    if first == 0:
        own, other = refs[:n_own], refs[n_own : 2 * n_own]
        state, u_ref, sems = refs[2 * n_own :]
        z, core, c = place[0], place[1], place[2]
        rows = own[0].shape[0] // n_z
        copies = []
        for k, half in ((core, own), (1 - core, other)):
            for m, part in enumerate(half):
                for s in range(n_z):
                    zz = lax.rem(z - s + n_z, n_z)
                    at = ((zz * 2 + k) * n_own + lax.bitwise_xor(c, m)) * rows
                    copies.append(
                        pltpu.make_async_copy(
                            part.at[pl.ds(s * rows, rows), :],
                            state.at[pl.ds(pl.multiple_of(at, rows), rows), :],
                            sems.at[len(copies)],
                        )
                    )
        for copy in copies:
            copy.start()
        u_ref[...] = jnp.zeros_like(u_ref)
        for copy in copies:
            copy.wait()
    else:
        state_in, u_in, state, u_ref = refs
        state[...] = state_in[...]
        u_ref[...] = u_in[...]
    n_blocks = state.shape[0] // LANES

    def step(p, _):
        block_step(p, n_blocks, state, u_ref)
        return 0

    lax.fori_loop(first, last, step, 0)


def cholesky_start(token, place, own, other, tile, last, n_z):
    return call(
        functools.partial(cholesky_kernel, 0, last, len(own), n_z),
        [f32(tile, tile)] * 2,
        [SMEM] + [ANY] * (2 * len(own)),
        [VMEM] * 2,
        [pltpu.SemaphoreType.DMA((2 * len(own) * n_z,))],
        limit=8 << 20,
        micros=60,
    )(token, place, *own, *other)


def cholesky_next(token, place, state, first, last):
    return call(
        functools.partial(cholesky_kernel, first, last, 0, 0),
        [f32(*state[0].shape)] * 2,
        [SMEM, VMEM, VMEM],
        [VMEM] * 2,
        limit=8 << 20,
        micros=20,
    )(token, place, *state)


def weights_kernel(place, state, u_ref, *refs):
    n_parts = len(refs) - 6
    parts = refs[:n_parts]
    x_high, x_low, w_high, w_low, own_l, lower = refs[n_parts:]
    tile = state.shape[0]
    z, core, c = place[0], place[1], place[2]
    r = lax.broadcasted_iota(jnp.int32, (tile, tile), 0)
    s = lax.broadcasted_iota(jnp.int32, (tile, tile), 1)
    w = jnp.where(s <= r, state[...], 0.0)
    w_parts = split(w)
    w_high[...], w_low[...] = split(w.T)
    panel = jnp.concatenate([parts[i][...] + parts[i + 1][...] for i in range(0, n_parts, 2)], 0)
    g = dot3(split(panel), w_parts, (((1,), (1,)), ((), ())))
    x_high[...], x_low[...] = split(dot3(split(g), w_parts))
    part_rows = own_l.shape[0]
    lower[...] = u_ref[...].T
    own_l[...] = lower[pl.ds(pl.multiple_of((z * 2 + core) * part_rows, part_rows), part_rows), :]


def weights(token, place, state, upper, parts, part_rows):
    tile = state.shape[0]
    total = sum(part.shape[0] for part in parts) // 2
    return call(
        weights_kernel,
        [bf16(total, tile)] * 2 + [bf16(tile, tile)] * 2 + [f32(part_rows, tile)],
        [SMEM] + [VMEM] * (2 + len(parts)),
        [VMEM] * 5,
        [pltpu.VMEM((tile, tile), jnp.float32)],
    )(token, place, state, upper, *parts)


def own_columns(row0, fac, at, part_rows):
    col_tiles, depth = row0.shape[0], row0.shape[1]
    for t in range(col_tiles):
        fac[t, :, 0:depth] = row0[t].T
    return fac[:, pl.ds(at, part_rows), 0:depth].reshape(col_tiles * part_rows, depth)


def update_kernel(chunks, starts, n_hops, place, gram, x_high, x_low, w_high, w_low, own_l, *refs):
    sources, rest = refs[: 1 + 2 * n_hops], refs[1 + 2 * n_hops :]
    trailing, factor, row0, old, new, zero, fac, prod, block_sems, old_sems, new_sems, zero_sems, fac_sem = rest[-13:]
    z, core, c = place[0], place[1], place[2]
    n_z = n_hops + 1
    _, cores, col_tiles, part_rows, lanes = sources[0].shape
    count, tile = old.shape[1], row0.shape[2]
    first_col = c == 0
    x = (x_high[...], x_low[...])

    def transfers(i):
        position, q = chunks[i]
        slot, here = i % 2, pl.ds(q * lanes, lanes)
        jobs = [(None, 0, z)]
        for s in range(1, n_hops + 1):
            for below, zz, inside in ((0, z - s, z >= s), (1, z + s, z + s < n_z)):
                jobs.append((inside & (core == below), s, zz))
                jobs.append((inside & (core != below), n_hops + s, zz))
        found = [(None, pltpu.make_async_copy(gram.at[pl.ds(1, count), :, :, here], old.at[slot], old_sems.at[slot]))]
        for job, (condition, source, zz) in enumerate(jobs):
            for k in range(cores):
                at = pl.multiple_of((zz * cores + k) * part_rows, part_rows)
                origin = sources[source].at[position - starts[source], k]
                target = row0.at[slot, :, pl.ds(at, part_rows), :]
                found.append((condition, pltpu.make_async_copy(origin, target, block_sems.at[slot, job, k])))
        return found

    def each(i, action):
        for condition, copy in transfers(i):
            if condition is None:
                action(copy)
            else:
                pl.when(condition)(functools.partial(action, copy))

    each(0, lambda copy: copy.start())
    zero[...] = jnp.zeros(zero.shape, jnp.float32)
    zeros = [
        pltpu.make_async_copy(zero, trailing.at[0, :, :, pl.ds(q * lanes, lanes)], zero_sems.at[i])
        for i, (_, q) in enumerate(chunks)
    ]
    outs = []
    mine = (z * cores + core) * part_rows
    place_factor = pltpu.make_async_copy(fac.at[:, pl.ds(0, part_rows), :], factor.at[:, 0], fac_sem)
    owner = [mine // lanes == q for _, q in chunks]
    for i, (_, q) in enumerate(chunks):
        slot, here = i % 2, pl.ds(q * lanes, lanes)
        if i + 1 < len(chunks):
            each(i + 1, lambda copy: copy.start())
        each(i, lambda copy: copy.wait())
        if i == 0:
            for copy in zeros:
                copy.start()
        if i >= 2:
            outs[i - 2].wait()
        for t in range(0, col_tiles, 2):
            column = split(jnp.concatenate([row0[slot, t], row0[slot, t + 1]], axis=1))
            product = dot3(x, column)
            prod[t] = product[:, :LANES]
            prod[t + 1] = product[:, LANES:]
        sub = lax.broadcasted_iota(jnp.int32, (part_rows, col_tiles, LANES), 1)
        for a in range(count):
            part = jnp.swapaxes(prod[:, a * part_rows : (a + 1) * part_rows, :], 0, 1)
            new[slot, a] = jnp.where(first_col & (sub == 0), 0.0, old[slot, a] - part)
        outs.append(
            pltpu.make_async_copy(new.at[slot], trailing.at[pl.ds(1, count), :, :, here], new_sems.at[slot])
        )
        outs[i].start()

        @pl.when(owner[i])
        def _():
            at = pl.multiple_of(mine % lanes, part_rows)
            across = own_columns(row0.at[slot], fac, at, part_rows)
            value = dot3(split(across), (w_high[...], w_low[...])).reshape(col_tiles, part_rows, tile)
            fac[:, 0:part_rows, :] = value
            fac[0, 0:part_rows, :] = jnp.where(first_col, own_l[...], value[0])
            place_factor.start()

    for is_owner in owner:
        pl.when(is_owner)(place_factor.wait)
    for copy in outs[-2:] + zeros:
        copy.wait()


def update(token, chunks, place, gram, weight, sources, previous):
    slab, part_rows, col_tiles, tile = gram.shape
    n_hops = (len(sources) - 1) // 2
    count = slab - 1
    operands = [place, gram, *weight, *(array for array, _ in sources)]
    specs = [SMEM, HBM] + [VMEM] * 5 + [ANY] * len(sources)
    aliases = {}
    if previous is not None:
        aliases = {len(operands): 0, len(operands) + 1: 1}
        operands += list(previous)
        specs += [HBM] * 2
    slots = pltpu.VMEM((2, count, part_rows, col_tiles, LANES), jnp.float32)
    scratch = [
        pltpu.VMEM((2, col_tiles, tile, LANES), jnp.float32),
        slots,
        slots,
        pltpu.VMEM((part_rows, col_tiles, LANES), jnp.float32),
        pltpu.VMEM((col_tiles, LANES, tile), jnp.float32),
        pltpu.VMEM((col_tiles, count * part_rows, LANES), jnp.float32),
        pltpu.SemaphoreType.DMA((2, 1 + 4 * n_hops, 2)),
        pltpu.SemaphoreType.DMA((2,)),
        pltpu.SemaphoreType.DMA((2,)),
        pltpu.SemaphoreType.DMA((len(chunks),)),
        pltpu.SemaphoreType.DMA,
    ]
    return call(
        functools.partial(update_kernel, chunks, [start for _, start in sources], n_hops),
        [f32(*gram.shape), f32(col_tiles, 1, part_rows, tile)],
        specs,
        [HBM, HBM],
        scratch,
        limit=26 << 20,
        micros=0,
        aliases=aliases,
    )(token, *operands)


def scatter(parts, root, axis):
    here = lax.axis_index(axis) == root
    mine = jnp.where(here, parts[0], 0.0)
    sent = [lax.ppermute(part, axis, [(root, i)]) for i, part in enumerate(parts) if i != root]
    return functools.reduce(jnp.add, sent, mine)


def exchange(part, axis, size):
    return [part] + [lax.ppermute(part, axis, [(i, i ^ m) for i in range(size)]) for m in range(1, size)]


def together(*values):
    return lax.optimization_barrier(values)


def body(gram, rows, cols):
    slab, part_rows, col_tiles, tile = gram.shape
    n_z = rows // 2
    n_chunks = tile // LANES
    n_blocks = tile // LANES
    core = lax.axis_index("row") % 2
    place = jnp.stack([lax.axis_index("row") // 2, core, lax.axis_index("col")]).astype(jnp.int32)
    other_core = [(i, i ^ 1) for i in range(rows)]
    swap = lambda value: lax.ppermute(value, "row", other_core)
    spread = lambda value, level: lax.ppermute(value, "col", [(i, i + level) for i in range(level)])

    def hop(value, s):
        pairs = [(2 * z, 2 * z + 2) for z in range(s - 1, n_z - 1)]
        pairs += [(2 * z + 1, 2 * z - 1) for z in range(1, n_z - s + 1)]
        return lax.ppermute(value, "row", pairs)

    order = sorted(range(n_chunks), key=lambda q: -abs(2 * q - n_chunks + 1))
    token = jnp.zeros((SUBLANES, LANES), jnp.float32)
    chunks, diagonal, token = prepare(token, gram[0], order)
    share = part_rows // cols
    piece = scatter([diagonal[i * share : (i + 1) * share] for i in range(cols)], 0, "col")
    partner = swap(chunks)
    blocks = jnp.stack([jnp.where(core == 0, chunks, partner), jnp.where(core == 0, partner, chunks)], 1)

    piece, blocks, token = together(piece, blocks, token)
    ring = [piece]
    for s in range(1, n_z):
        ring.append(lax.ppermute(piece, "row", [(i, (i + 2 * s) % rows) for i in range(rows)]))
    piece = jnp.concatenate(ring, 0)
    panel, token = take_panel(token, place, gram)
    panel = panel.reshape((slab - 1) * part_rows, tile)
    levels = cols.bit_length() - 1
    piece, blocks, token = together(piece, blocks, token)
    hops = [hop(blocks, 1)]
    halves = exchange(piece, "col", cols)
    panel, *halves = together(panel, *halves)
    others = [swap(half) for half in halves]

    height = panel.shape[0]
    bounds = [0, height * 2 // 5 // SUBLANES * SUBLANES, height * 3 // 4 // SUBLANES * SUBLANES, height]
    held = [panel[first:last] for first, last in zip(bounds[:-1], bounds[1:])]
    sent = [None] * len(held)

    def launch(step):
        moving = [i for i in range(len(held)) if 0 <= step - i < levels]
        for i in moving:
            if step > i:
                held[i] = held[i] + sent[i]
            sent[i] = spread(held[i], 1 << (step - i))
        return moving

    for p in range(n_blocks):
        moving = launch(p)
        if p == 0:
            *state, token = cholesky_start(token, place, halves, others, tile, 1, n_z)
        else:
            if p == n_blocks - 1:
                token, *hops = together(token, *hops)
            *state, token = cholesky_next(token, place, state, p, p + 1)
        if p == 0:
            token, hops[0], sent[0] = together(token, hops[0], sent[0])
            for s in range(2, n_z - 1):
                hops.append(hop(hops[-1], s))
        else:
            token, *landed = together(token, *(sent[i] for i in moving))
            for i, value in zip(moving, landed):
                sent[i] = value
    for step in range(n_blocks, len(held) + levels - 1):
        launch(step)
    parts = [value for pair in zip(held, sent) for value in pair]
    swapped = [swap(value) for value in hops]

    pair = n_chunks // 2
    finals = [hop(hops[-1][i : i + pair], n_z - 1) for i in (0, pair)]
    *weight, token = weights(token, place, *state, parts, part_rows)
    outs = None
    for final, first in zip(finals, (0, pair)):
        token, final = together(token, final)
        sources = [(value, 0) for value in (blocks, *hops)] + [(final, first)]
        sources += [(value, 0) for value in swapped] + [(swap(final), first)]
        positions = [(i, order[i]) for i in range(first, first + pair)]
        *outs, token = update(token, positions, place, gram, weight, sources, outs)
    return tuple(outs)


def solution(mesh):
    rows, cols = mesh.shape["row"], mesh.shape["col"]
    return jax.shard_map(
        functools.partial(body, rows=rows, cols=cols),
        mesh=mesh,
        in_specs=(P(None, "row", None, "col"),),
        out_specs=(P(None, "row", None, "col"), P(None, "col", "row", None)),
        check_vma=False,
    )
```
